32 devices in a mesh: parts: 2 (over x), tm: 2 (over core), node: 8 (over z, y).
Axes of the slice: x: 2, y: 2, z: 4, core: 2. Of those that a mesh axis runs over, the one named last changes fastest.
Arguments:
- initial_fields: float32 [4, 32768], P('parts', 'node'), parts along dimension 0, may hold values from 0 to 1
- feed_rate: float32 [32768], P('node'), may hold values from 0.05 to 0.5
- kill_rate: float32 [32768], P('node'), may hold values from 0.05 to 1
- fine_tiles: float32 [256, 3, 128, 128], P('node'), may hold values from -0.3125 to 0.3125
- fine_cols: int32 [256, 3], P('node'), may hold values from 0 to 55, as said below
- fine_halo: int32 [24576], P('node'), may hold values from 0 to 4095, as said below
- coarse_tiles: float32 [64, 3, 128, 128], P('node'), may hold values from -0.3125 to 0.3125
- coarse_cols: int32 [64, 3], P('node'), may hold values from 0 to 13, as said below
- coarse_halo: int32 [6144], P('node'), may hold values from 0 to 1023, as said below
- children: int32 [32768], P('node'), may hold values from 0 to 4095, as said below
Outputs:
- final_states: float32 [8, 4, 32768], P('tm', 'parts', 'node'), parts along dimension 1
The draws below stay inside these ranges and needn't reach their ends.
There are 2 independent parts, one for each index of `parts`. The reference program is written for one: setup_inputs(seed, part) draws one part's arguments, and reference() takes and returns one part's arrays. A program takes and returns all parts, laid end to end along the dimension named above; an argument that names none is the same for every part. Nothing has to cross between parts.
Inputs may be any that keep to these rules, and one draw needn't show every extreme that they name: `fine_cols`: entry 0 of row block r of a band is 12 + r, its own block; the others lie within 12 blocks of it. Blocks are counted over the extended rows: 12 halo blocks from the band below, the band's 32 own blocks, then 12 halo blocks from the band above. The lowest band names no block under 12, the highest none at 44 or above. `coarse_cols`: entry 0 of coarse row block r of a band is 3 + r; the others lie within 3 blocks of it, counted as for fine_cols with 3 halo blocks on each side and 8 own blocks. The lowest band names no block under 3, the highest none at 11 or above. `fine_halo`: each band has 3072 entries, rows of that band: the first 1536 are distinct rows under 2 * 1536, row 0 among them; the last 1536 are distinct rows at 1024 or above, the band's last row among them. `coarse_halo`: each band has 768 entries, coarse rows of that band: the first 384 are distinct rows under 2 * 384, row 0 among them; the last 384 are distinct rows at 256 or above, the band's last row among them. `children`: the 4096 entries of each band are a permutation of its rows 0 to 4095.
All inputs are finite; a program needn't handle non-finite values.
Results may differ from the reference program's by a relative error of at most 0.0001.
Values sent between devices are 32-bit elements; how exact they have to be, the bound alone decides.
A program may use at most 128 MiB of HBM per device.

```python
import math
import jax
import jax.numpy as jnp
from jax import lax

TILE = 128
STENCIL = 3
NB = 32
HB = 12
NBC = 8
HBC = 3
NODES_DEV = 4096
NODES = 32768
COARSE_DEV = 1024
HALO = 1536
HALO_C = 384
SLICES = 8
ITERS = 2
N_NODE = 8


def block_columns(key, blocks, halo_blocks, stencil, band_count):
    total_rows = band_count * blocks
    band_index = jnp.arange(total_rows, dtype=jnp.int32) // blocks
    within = jnp.arange(total_rows, dtype=jnp.int32) % blocks
    magnitude = jax.random.randint(jax.random.fold_in(key, 101), (total_rows, stencil - 1), 1, halo_blocks + 1)
    direction = jax.random.randint(jax.random.fold_in(key, 102), (total_rows, stencil - 1), 0, 2) * 2 - 1
    offset = magnitude * direction
    own_block = halo_blocks + within
    target = own_block[:, None] + offset
    mirror = own_block[:, None] - offset
    too_low = (band_index[:, None] == 0) & (target < halo_blocks)
    too_high = (band_index[:, None] == band_count - 1) & (target >= halo_blocks + blocks)
    target = jnp.where(too_low | too_high, mirror, target)
    lowest_row = (within == 0) & (band_index > 0)
    highest_row = (within == blocks - 1) & (band_index < band_count - 1)
    first_other = jnp.where(lowest_row, 0, target[:, 0])
    last_other = jnp.where(highest_row, 2 * halo_blocks + blocks - 1, target[:, -1])
    target = target.at[:, 0].set(first_other)
    target = target.at[:, -1].set(last_other)
    return jnp.concatenate([own_block[:, None], target], axis=1).astype(jnp.int32)


def halo_picks(key, rows_band, halo_rows, band_count):
    subkeys = jax.random.split(key, 2 * band_count)

    def single_list(subkey):
        others = jax.random.permutation(subkey, 2 * halo_rows - 1)[:halo_rows - 1] + 1
        return jnp.concatenate([jnp.zeros((1,), jnp.int32), others.astype(jnp.int32)])
    chosen = jax.vmap(single_list)(subkeys).reshape((band_count, 2, halo_rows))
    below_rows = chosen[:, 0]
    above_rows = rows_band - 1 - chosen[:, 1]
    return jnp.concatenate([below_rows, above_rows], axis=1).reshape((-1,)).astype(jnp.int32)


def draw_fine_cols(key, part):
    key = jax.random.fold_in(key, 1)
    return block_columns(key, NB, HB, STENCIL, N_NODE)


def draw_fine_halo(key, part):
    key = jax.random.fold_in(key, 2)
    return halo_picks(key, NODES_DEV, HALO, N_NODE)


def draw_coarse_cols(key, part):
    key = jax.random.fold_in(key, 3)
    return block_columns(key, NBC, HBC, STENCIL, N_NODE)


def draw_coarse_halo(key, part):
    key = jax.random.fold_in(key, 4)
    return halo_picks(key, COARSE_DEV, HALO_C, N_NODE)


def draw_children(key, part):
    key = jax.random.fold_in(key, 5)
    subkeys = jax.random.split(key, N_NODE)
    orders = jax.vmap(lambda subkey: jax.random.permutation(subkey, NODES_DEV))(subkeys)
    return orders.reshape((-1,)).astype(jnp.int32)


def block_levels(stream_key, extent, shards, low, high):
    loudness = 1.0
    for position, blocks in shards:
        draws = jax.random.uniform(jax.random.fold_in(jax.random.fold_in(stream_key, 6), position), (blocks,), jnp.float32, low / len(shards), high / len(shards))
        loudness = loudness * jnp.repeat(jnp.exp(draws), extent[position] // blocks).reshape((-1,) + (1,) * (len(extent) - 1 - position))
    return loudness


def gaussian(stream_key, dims, deviation, bound, shards=(), kind=jnp.bfloat16):
    array = jax.random.normal(stream_key, dims, jnp.float32) * deviation
    if len(shards) > 0:
        array = block_levels(stream_key, dims, shards, -0.22, 0.18) * array
    return jnp.clip(array, min=-bound, max=bound).astype(kind)


def setup_inputs(seed: int = 0, part: int = 0) -> dict:
    keys = jax.random.split(jax.random.key(seed), 11)
    own_keys = jax.random.split(jax.random.fold_in(keys[10], part), 11)
    return {
        "initial_fields": jnp.clip(1.0 * jax.random.uniform(own_keys[0], (2, NODES), jnp.float32) ** block_levels(own_keys[0], (2, NODES), ((1, 8),), -0.2, 0.2), 0.0, 1.0),
        "feed_rate": jnp.clip(jnp.exp(math.log(0.5) - 2.3025851 * jax.random.uniform(keys[1], (NODES,), jnp.float32) ** block_levels(keys[1], (NODES,), ((0, 8),), -0.2, 0.2)), 0.05, 0.5),
        "kill_rate": jnp.clip(jnp.exp(math.log(1.0) - 2.9957323 * jax.random.uniform(keys[2], (NODES,), jnp.float32) ** block_levels(keys[2], (NODES,), ((0, 8),), -0.2, 0.2)), 0.05, 1.0),
        "fine_tiles": gaussian(keys[3], (N_NODE * NB, STENCIL, TILE, TILE), (STENCIL * TILE) ** -0.5, 0.3125, ((0, 8),), jnp.float32),
        "fine_cols": draw_fine_cols(jax.random.fold_in(keys[10], 71), part),
        "fine_halo": draw_fine_halo(jax.random.fold_in(keys[10], 71), part),
        "coarse_tiles": gaussian(keys[6], (N_NODE * NBC, STENCIL, TILE, TILE), (STENCIL * TILE) ** -0.5, 0.3125, ((0, 8),), jnp.float32),
        "coarse_cols": draw_coarse_cols(jax.random.fold_in(keys[10], 71), part),
        "coarse_halo": draw_coarse_halo(jax.random.fold_in(keys[10], 71), part),
        "children": draw_children(jax.random.fold_in(keys[10], 71), part),
    }


highest = lax.Precision.HIGHEST
diffusion_u = 1.0
diffusion_v = 0.5
self_weight = 1.5
slice_step = 0.25
half_step = 0.125
quad_rows = ((5.0 / 24.0, 1.0 / 3.0, -1.0 / 24.0), (-1.0 / 24.0, 1.0 / 3.0, 5.0 / 24.0))


def band_apply(field, tiles, columns, rim_rows):
    band_count = N_NODE
    tile_size = tiles.shape[-1]
    leading = field.shape[:-1]
    flattened = field.reshape((-1, band_count, field.shape[-1] // band_count))
    rim_table = rim_rows.reshape((band_count, -1))
    rim_width = rim_table.shape[1] // 2
    sent_rows = jax.vmap(lambda band_part, band_rows: band_part[:, band_rows], in_axes=(1, 0), out_axes=1)(flattened, rim_table)
    zero_rim = jnp.zeros((sent_rows.shape[0], 1, rim_width), sent_rows.dtype)
    below_rim = jnp.concatenate([zero_rim, sent_rows[:, :-1, rim_width:]], axis=1)
    above_rim = jnp.concatenate([sent_rows[:, 1:, :rim_width], zero_rim], axis=1)
    extended = jnp.concatenate([below_rim, flattened, above_rim], axis=2)
    extended = extended.reshape((extended.shape[0], band_count, -1, tile_size))
    block_lists = columns.reshape((band_count, -1, columns.shape[-1]))
    picked = jax.vmap(lambda band_part, band_blocks: band_part[:, band_blocks], in_axes=(1, 0), out_axes=1)(extended, block_lists)
    weights = tiles.reshape((band_count, -1) + tiles.shape[1:])
    combined = jnp.einsum("dbsij,cdbsj->cdbi", weights, picked, precision=highest)
    return combined.reshape(leading + (field.shape[-1],)) - self_weight * field


def restrict(field, children):
    band_count = N_NODE
    flattened = field.reshape((-1, band_count, field.shape[-1] // band_count))
    orders = children.reshape((band_count, -1))
    taken = jax.vmap(lambda band_part, band_rows: band_part[:, band_rows], in_axes=(1, 0), out_axes=1)(flattened, orders)
    summed = taken.reshape(taken.shape[:2] + (-1, 4)).sum(axis=-1) * 0.25
    return summed.reshape(field.shape[:-1] + (-1,))


def prolong(coarse, children):
    band_count = N_NODE
    flattened = coarse.reshape((-1, band_count, coarse.shape[-1] // band_count))
    orders = children.reshape((band_count, -1))
    spread = jnp.repeat(flattened, 4, axis=-1)
    placed = jax.vmap(lambda band_part, band_rows: jnp.zeros_like(band_part).at[:, band_rows].set(band_part), in_axes=(1, 0), out_axes=1)(spread, orders)
    return placed.reshape(coarse.shape[:-1] + (-1,))


def explicit(state, laplacian, source):
    growth = state[..., 0, :] * state[..., 1, :] * state[..., 1, :]
    first_row = diffusion_u * laplacian[..., 0, :] - growth + source
    second_row = diffusion_v * laplacian[..., 1, :] + growth
    return jnp.stack([first_row, second_row], axis=-2)


def advance(previous, terms_new, terms_old, old_next, decay, integral, defect):
    return (previous + half_step * (terms_new - terms_old) + half_step * decay * old_next + integral + defect) / (1.0 + half_step * decay)


def quadrature(values):
    pieces = []
    for weights in quad_rows:
        pieces.append(slice_step * (weights[0] * values[..., 0, :, :] + weights[1] * values[..., 1, :, :] + weights[2] * values[..., 2, :, :]))
    return jnp.stack(pieces, axis=-3)


def run_chain(first_value, coarse_nodes, coarse_values, coarse_quad, defects, coarse_terms, coarse_decay):
    def advance_slice(current, inputs):
        node_values, term_values, quad_values, defect = inputs
        node_one = advance(current, coarse_terms(current), term_values[0], node_values[1], coarse_decay, quad_values[0], defect[0])
        node_two = advance(node_one, coarse_terms(node_one), term_values[1], node_values[2], coarse_decay, quad_values[1], defect[1])
        return node_two, jnp.stack([node_one, node_two])

    final_state, results = lax.scan(advance_slice, first_value, (coarse_nodes, coarse_values, coarse_quad, defects))
    return results


def reference(initial_fields, feed_rate, kill_rate, fine_tiles, fine_cols, fine_halo, coarse_tiles, coarse_cols, coarse_halo, children):
    decay = jnp.stack([feed_rate, feed_rate + kill_rate])
    coarse_decay = restrict(decay, children)

    def fine_terms(state):
        return explicit(state, band_apply(state, fine_tiles, fine_cols, fine_halo), feed_rate)

    def coarse_terms(state):
        return explicit(state, band_apply(state, coarse_tiles, coarse_cols, coarse_halo), coarse_decay[0])

    base = restrict(initial_fields, children)
    base_terms = coarse_terms(base)
    base_values = base_terms - coarse_decay * base
    base_quad = quadrature(jnp.stack([base_values, base_values, base_values]))
    node_shape = (SLICES, 3) + base.shape
    results = run_chain(base, jnp.broadcast_to(base, node_shape), jnp.broadcast_to(base_terms, node_shape),
                        jnp.broadcast_to(base_quad, (SLICES, 2) + base.shape),
                        jnp.zeros((SLICES, 2) + base.shape, base.dtype), coarse_terms, coarse_decay)
    states = initial_fields + prolong(results - base, children)
    initial_terms = fine_terms(initial_fields)

    for iteration in range(ITERS):
        pair_terms = fine_terms(states)
        start_nodes = jnp.concatenate([initial_fields[None], states[:-1, 1]], axis=0)
        start_terms = jnp.concatenate([initial_terms[None], pair_terms[:-1, 1]], axis=0)
        node_values = jnp.stack([start_nodes, states[:, 0], states[:, 1]], axis=1)
        term_values = jnp.stack([start_terms, pair_terms[:, 0], pair_terms[:, 1]], axis=1)
        fine_quad = quadrature(term_values - decay * node_values)
        node_one = advance(node_values[:, 0], term_values[:, 0], term_values[:, 0], node_values[:, 1], decay, fine_quad[:, 0], 0.0)
        terms_one = fine_terms(node_one)
        node_two = advance(node_one, terms_one, term_values[:, 1], node_values[:, 2], decay, fine_quad[:, 1], 0.0)
        terms_two = fine_terms(node_two)
        swept = jnp.stack([node_values[:, 0], node_one, node_two], axis=1)
        swept_terms = jnp.stack([term_values[:, 0], terms_one, terms_two], axis=1)
        coarse_nodes = restrict(swept, children)
        coarse_values = coarse_terms(coarse_nodes)
        coarse_parts = coarse_values - coarse_decay * coarse_nodes
        coarse_quad = quadrature(coarse_parts)
        defects = quadrature(restrict(swept_terms - decay * swept, children) - coarse_parts)
        results = run_chain(coarse_nodes[0, 0], coarse_nodes, coarse_values, coarse_quad, defects, coarse_terms, coarse_decay)
        states = swept[:, 1:] + prolong(results - coarse_nodes[:, 1:], children)
    return states[:, 1]
```

```python
import functools
import jax
import jax.numpy as jnp
from jax import lax
from jax.experimental import pallas as pl
from jax.experimental.pallas import tpu as pltpu
from jax.sharding import PartitionSpec as P

SLICES = 8
ITERS = 2
LANES = 128
ROWS = 8
DT = 0.125
QUAD = ((5.0 / 96.0, 1.0 / 12.0, -1.0 / 96.0), (-1.0 / 96.0, 1.0 / 12.0, 5.0 / 96.0))

f32 = jnp.float32
bf16 = jnp.bfloat16


def take(block, lane):
    return jnp.take_along_axis(block, lane, axis=1, mode="promise_in_bounds")


def species_mask():
    return lax.broadcasted_iota(jnp.int32, (ROWS, LANES), 0) < ROWS // 2


def explicit(x, product, source):
    is_u = species_mask()
    other = pltpu.roll(x, ROWS // 2, 0)
    growth = x * other * jnp.where(is_u, other, x)
    laplacian = product - 1.5 * x
    return jnp.where(is_u, laplacian - growth, 0.5 * laplacian + growth) + source


class Level:
    def __init__(self, count, rim, cols, weights, rim_index):
        self.count = count
        self.rim = rim
        self.cols = cols
        self.weights = weights
        self.rim_index = rim_index


def rim_copies(level, ext, send, send_sem, recv_sem, node):
    rim, count = level.rim, level.count
    down = pltpu.make_async_remote_copy(
        src_ref=send.at[pl.ds(0, rim)],
        dst_ref=ext.at[pl.ds(rim + count, rim)],
        send_sem=send_sem.at[0],
        recv_sem=recv_sem.at[0],
        device_id={"node": node - 1},
        device_id_type=pl.DeviceIdType.MESH,
    )
    up = pltpu.make_async_remote_copy(
        src_ref=send.at[pl.ds(rim, rim)],
        dst_ref=ext.at[pl.ds(0, rim)],
        send_sem=send_sem.at[1],
        recv_sem=recv_sem.at[1],
        device_id={"node": node + 1},
        device_id_type=pl.DeviceIdType.MESH,
    )
    return down, up


def gather_rim(level, ext, send, side, groups):
    rim, count = level.rim, level.count
    reach = min(2 * rim, count)
    first = 0 if side == 0 else count - reach

    def body(step, carry):
        place = side * rim + step
        index = level.rim_index[place]
        lane = index & (LANES - 1)
        owner = index >> 7
        for group in range(groups):
            rows = pl.ds(group * ROWS, ROWS)
            found = take(ext[rim + first, rows, :], lane)
            for block in range(first + 1, first + reach):
                found = jnp.where(owner == block, take(ext[rim + block, rows, :], lane), found)
            send[place, rows, :] = found
        return carry

    if rim <= 3:
        for step in range(rim):
            body(step, 0)
    else:
        lax.fori_loop(0, rim, body, 0)


def operator(level, ext, send, send_sem, recv_sem, node, nodes, emit):
    groups = ext.shape[1] // ROWS
    rows = groups * ROWS
    down, up = rim_copies(level, ext, send, send_sem, recv_sem, node)
    gather_rim(level, ext, send, 0, groups)
    pl.when(node > 0)(lambda: down.start())
    gather_rim(level, ext, send, 1, groups)
    pl.when(node < nodes - 1)(lambda: up.start())
    pl.when(node < nodes - 1)(lambda: down.wait_recv())
    pl.when(node > 0)(lambda: up.wait_recv())

    def product(r):
        x = jnp.concatenate([ext[level.cols[3 * r + s]] for s in range(3)], axis=1)
        high = x.astype(bf16).astype(f32)
        both = jnp.concatenate([high, x - high], axis=0).astype(bf16)
        wide = jnp.dot(both, level.weights[r], preferred_element_type=f32)
        return wide[:rows, :LANES] + wide[:rows, LANES:] + wide[rows:, :LANES]

    if level.count <= 8:
        for r in range(level.count):
            emit(r, product(r))
    else:
        def body(r, carry):
            emit(r, product(r))
            return carry

        lax.fori_loop(0, level.count, body, 0, unroll=4)
    pl.when(node > 0)(lambda: down.wait_send())
    pl.when(node < nodes - 1)(lambda: up.wait_send())


def kernel(
    nodes,
    tms,
    cols_f,
    cols_c,
    init,
    rate,
    w_f,
    w_c,
    rim_f,
    rim_c,
    owners,
    mapping,
    out,
    ext_a,
    ext_b,
    ext_c,
    ext_d,
    ext_0,
    ext_1,
    send_a,
    send_b,
    send_c,
    send_d,
    send_0,
    send_1,
    send_sem,
    recv_sem,
    state,
    terms,
    lhs,
    coarse_rate,
    base,
    fixed,
    coarse_w,
    results,
    end_coarse,
    got_coarse,
    end_fine,
    got_fine,
    tm_send,
    tm_recv,
):
    node = lax.axis_index("node")
    tm = lax.axis_index("tm")
    per = ROWS // 2
    nb = init.shape[0]
    nbc = coarse_rate.shape[0]
    fine = Level(nb, rim_f.shape[0] // 2, cols_f, w_f, rim_f)
    coarse = Level(nbc, rim_c.shape[0] // 2, cols_c, w_c, rim_c)

    barrier = pltpu.get_barrier_semaphore()

    def greet(axis, position, size):
        for offset in (-1, 1):
            other = position + offset

            @pl.when((other >= 0) & (other < size))
            def _():
                pl.semaphore_signal(
                    barrier, inc=1, device_id={axis: other}, device_id_type=pl.DeviceIdType.MESH
                )

    greet("node", node, nodes)
    greet("tm", tm, tms)

    peers = sum(
        ((other >= 0) & (other < size)).astype(jnp.int32)
        for other, size in ((node - 1, nodes), (node + 1, nodes), (tm - 1, tms), (tm + 1, tms))
    )
    pl.semaphore_wait(barrier, peers)

    is_u = species_mask()
    row = lax.broadcasted_iota(jnp.int32, (ROWS, LANES), 0)
    slice_of = row & (per - 1)

    def restrict(pieces, write):
        count = len(pieces)

        def body(b, carry):
            lanes = pl.ds(pl.multiple_of(b * LANES, LANES), LANES)
            for g in range(count):
                x = pieces[g](b)
                high = x.astype(bf16).astype(f32)
                lhs[pl.ds(16 * g, 16), lanes] = jnp.concatenate([high, x - high], axis=0).astype(bf16)
            return carry

        lax.fori_loop(0, nb, body, 0, unroll=2)
        summed = jnp.dot(lhs[pl.ds(0, 16 * count), :], mapping[...], preferred_element_type=f32)
        for g in range(count):
            both = summed[16 * g : 16 * g + 8] + summed[16 * g + 8 : 16 * g + 16]
            for b in range(nbc):
                write(g, b, both[:, b * LANES : (b + 1) * LANES])

    def prolong(z, d):
        index = owners[d]
        lane = index & (LANES - 1)
        owner = index >> 7
        found = take(z[0], lane)
        for b in range(1, nbc):
            found = jnp.where(owner == b, take(z[b], lane), found)
        return found

    def coarse_source(b):
        return jnp.where(is_u, coarse_rate[b], 0.0)

    def fine_source(b):
        return jnp.where(is_u, rate[b], 0.0)

    def tm_copy(source, target, slot, sem):
        return pltpu.make_async_remote_copy(
            src_ref=source.at[slot],
            dst_ref=target.at[slot],
            send_sem=tm_send.at[sem],
            recv_sem=tm_recv.at[sem],
            device_id={"tm": tm + 1},
            device_id_type=pl.DeviceIdType.MESH,
        )

    def chain(number, start, has_fixed):
        copy = tm_copy(end_coarse, got_coarse, number, number)
        pl.when(tm > 0)(lambda: copy.wait_recv())
        for b in range(nbc):
            ext_0[coarse.rim + b] = jnp.where(tm == 0, start[b], got_coarse[number, b])

        def slice_body(s, carry):
            for m, (ext, send, sem, target) in enumerate(
                ((ext_0, send_0, 4, ext_1), (ext_1, send_1, 5, ext_0))
            ):
                def emit(b, product, m=m, ext=ext, target=target):
                    y = ext[coarse.rim + b]
                    value = y + DT * explicit(y, product, coarse_source(b))
                    if has_fixed:
                        value = value + fixed[m, b]
                    value = value / (1.0 + DT * coarse_rate[b])
                    results[m, b] = jnp.where(slice_of == s, value, results[m, b])
                    target[coarse.rim + b] = value if m == 0 else pltpu.roll(value, 1, 0)

                operator(coarse, ext, send, send_sem.at[sem], recv_sem.at[sem], node, nodes, emit)
            return carry

        lax.fori_loop(0, per, slice_body, 0)

        @pl.when(tm < tms - 1)
        def _():
            for b in range(nbc):
                end_coarse[number, b] = pltpu.roll(results[1, b], ROWS - (per - 1), 0)
            copy.start()

    def finish_chain(number):
        copy = tm_copy(end_coarse, got_coarse, number, number)
        pl.when(tm < tms - 1)(lambda: copy.wait_send())

    results[...] = jnp.zeros_like(results)
    for ext, rim in (
        (ext_a, fine.rim), (ext_b, fine.rim), (ext_c, fine.rim),
        (ext_d, coarse.rim), (ext_0, coarse.rim), (ext_1, coarse.rim),
    ):
        @pl.when(node == 0)
        def _(ext=ext, rim=rim):
            ext[pl.ds(0, rim)] = jnp.zeros((rim,) + ext.shape[1:], f32)

        @pl.when(node == nodes - 1)
        def _(ext=ext, rim=rim):
            ext[pl.ds(ext.shape[0] - rim, rim)] = jnp.zeros((rim,) + ext.shape[1:], f32)

    def write_base(g, b, value):
        if g == 0:
            coarse_rate[b] = value
        else:
            base[b] = value

    restrict([lambda b: rate[b], lambda b: init[b]], write_base)
    chain(0, base, False)
    finish_chain(0)

    def first_states(d, carry):
        for m in range(2):
            z = [results[m, b] - base[b] for b in range(nbc)]
            state[m, d] = init[d] + prolong(z, d)
        return carry

    lax.fori_loop(0, nb, first_states, 0)

    def iterate(it, carry):
        copy = tm_copy(end_fine, got_fine, it, 3 + it)

        @pl.when(tm < tms - 1)
        def _():
            def body(b, c):
                end_fine[it, b] = pltpu.roll(state[1, b], ROWS - (per - 1), 0)
                return c

            lax.fori_loop(0, nb, body, 0, unroll=4)
            copy.start()

        pl.when(tm > 0)(lambda: copy.wait_recv())

        def prepare(b, c):
            start = jnp.where(tm == 0, init[b], got_fine[it, b])
            last = state[1, b]
            place = fine.rim + b
            ext_a[place, 0:8] = jnp.where(slice_of == 0, start, pltpu.roll(last, 1, 0))
            ext_a[place, 8:16] = state[0, b]
            ext_a[place, 16:24] = last
            return c

        lax.fori_loop(0, nb, prepare, 0, unroll=4)

        def emit_a(r, product):
            place = fine.rim + r
            source = fine_source(r)
            decay = rate[r]
            u = [ext_a[place, 8 * m : 8 * m + 8] for m in range(3)]
            f = [explicit(u[m], product[8 * m : 8 * m + 8], source) for m in range(3)]
            g = [f[m] - decay * u[m] for m in range(3)]
            q = [sum(w * v for w, v in zip(weights, g)) for weights in QUAD]
            ext_b[place] = (u[0] + DT * decay * u[1] + q[0]) / (1.0 + DT * decay)
            terms[0, r] = g[0]
            terms[1, r] = DT * decay * u[2] + q[1] - DT * f[1]

        operator(fine, ext_a, send_a, send_sem.at[0], recv_sem.at[0], node, nodes, emit_a)
        pl.when(tm < tms - 1)(lambda: copy.wait_send())

        def emit_b(r, product):
            place = fine.rim + r
            decay = rate[r]
            v = ext_b[place]
            e = explicit(v, product, fine_source(r))
            ext_c[place] = (v + DT * e + terms[1, r]) / (1.0 + DT * decay)
            terms[1, r] = e - decay * v

        operator(fine, ext_b, send_b, send_sem.at[1], recv_sem.at[1], node, nodes, emit_b)

        def emit_c(r, product):
            v = ext_c[fine.rim + r]
            terms[2, r] = explicit(v, product, fine_source(r)) - rate[r] * v

        operator(fine, ext_c, send_c, send_sem.at[2], recv_sem.at[2], node, nodes, emit_c)

        def quad_piece(weights):
            return lambda b: sum(w * terms[m, b] for m, w in enumerate(weights))

        def write(g, b, value):
            if g < 2:
                ext_d[coarse.rim + b, 8 * g : 8 * g + 8] = value
            if g < 3:
                coarse_w[g, b] = value
            else:
                fixed[g - 3, b] = value

        restrict(
            [
                lambda b: ext_a[fine.rim + b, 0:8],
                lambda b: ext_b[fine.rim + b],
                lambda b: ext_c[fine.rim + b],
                quad_piece(QUAD[0]),
                quad_piece(QUAD[1]),
            ],
            write,
        )

        def emit_d(b, product):
            source = coarse_source(b)
            for m in range(2):
                e = explicit(coarse_w[m, b], product[8 * m : 8 * m + 8], source)
                fixed[m, b] = fixed[m, b] + DT * (coarse_rate[b] * coarse_w[m + 1, b] - e)

        operator(coarse, ext_d, send_d, send_sem.at[3], recv_sem.at[3], node, nodes, emit_d)
        chain(1 + it, coarse_w.at[0], True)
        finish_chain(1 + it)

        def new_states(d, c):
            z = [results[1, b] - coarse_w[2, b] for b in range(nbc)]
            state[1, d] = ext_c[fine.rim + d] + prolong(z, d)
            z = [results[0, b] - coarse_w[1, b] for b in range(nbc)]
            state[0, d] = ext_b[fine.rim + d] + prolong(z, d)
            return c

        lax.fori_loop(0, nb, new_states, 0)
        return carry

    lax.fori_loop(0, ITERS, iterate, 0)
    out[...] = state[1]


def spread(u, v, per):
    pieces = [u.reshape((-1, 1, LANES))] * per + [v.reshape((-1, 1, LANES))] * per
    return jnp.concatenate(pieces, axis=1)


def weight_parts(tiles):
    flipped = tiles.transpose((0, 1, 3, 2)).reshape((tiles.shape[0], -1, LANES))
    high = lax.reduce_precision(flipped, 8, 7)
    return jnp.concatenate([high.astype(bf16), (flipped - high).astype(bf16)], axis=2)


def per_device(
    nodes,
    tms,
    initial_fields,
    feed_rate,
    kill_rate,
    fine_tiles,
    fine_cols,
    fine_halo,
    coarse_tiles,
    coarse_cols,
    coarse_halo,
    children,
):
    per = SLICES // tms
    nb, nbc = fine_tiles.shape[0], coarse_tiles.shape[0]
    hb, hbc = fine_halo.shape[0] // (2 * LANES), coarse_halo.shape[0] // (2 * LANES)
    count = children.shape[0]
    init = spread(initial_fields[0], initial_fields[1], per)
    rate = spread(feed_rate, feed_rate + kill_rate, per)

    ordinal = jnp.arange(count, dtype=jnp.int32) // 4
    in_block = (children // LANES)[None, :] == jnp.arange(nb, dtype=jnp.int32)[:, None]
    left = jnp.concatenate(
        [jnp.where(in_block, ordinal // 32, 0), jnp.where(in_block, ordinal % 32, 0)], axis=0
    ).astype(bf16)
    right = (
        (children % LANES)[:, None] == jnp.arange(LANES, dtype=jnp.int32)[None, :]
    ).astype(bf16)
    halves = jnp.dot(left, right, preferred_element_type=f32).astype(jnp.int32)
    owner = halves[:nb] * 32 + halves[nb:]
    mapping = jnp.where(
        owner.reshape((-1, 1)) == jnp.arange(count // 4, dtype=jnp.int32)[None, :], 0.25, 0.0
    ).astype(bf16)

    def widen(index):
        return jnp.broadcast_to(index.reshape((-1, 1, LANES)), (index.size // LANES, ROWS, LANES))

    vmem = pl.BlockSpec(memory_space=pltpu.VMEM)
    smem = pl.BlockSpec(memory_space=pltpu.SMEM)
    fine_ext, coarse_ext = nb + 2 * hb, nbc + 2 * hbc

    def scratch(*shape):
        return pltpu.VMEM(shape + (LANES,), f32)

    result = pl.pallas_call(
        functools.partial(kernel, nodes, tms),
        out_shape=jax.ShapeDtypeStruct((nb, ROWS, LANES), f32),
        in_specs=[smem, smem] + [vmem] * 8,
        out_specs=vmem,
        scratch_shapes=[
            scratch(fine_ext, 24),
            scratch(fine_ext, 8),
            scratch(fine_ext, 8),
            scratch(coarse_ext, 16),
            scratch(coarse_ext, 8),
            scratch(coarse_ext, 8),
            scratch(2 * hb, 24),
            scratch(2 * hb, 8),
            scratch(2 * hb, 8),
            scratch(2 * hbc, 16),
            scratch(2 * hbc, 8),
            scratch(2 * hbc, 8),
            pltpu.SemaphoreType.DMA((6, 2)),
            pltpu.SemaphoreType.DMA((6, 2)),
            scratch(2, nb, ROWS),
            scratch(3, nb, ROWS),
            pltpu.VMEM((80, count), bf16),
            scratch(nbc, ROWS),
            scratch(nbc, ROWS),
            scratch(2, nbc, ROWS),
            scratch(3, nbc, ROWS),
            scratch(2, nbc, ROWS),
            scratch(1 + ITERS, nbc, ROWS),
            scratch(1 + ITERS, nbc, ROWS),
            scratch(ITERS, nb, ROWS),
            scratch(ITERS, nb, ROWS),
            pltpu.SemaphoreType.DMA((1 + 2 * ITERS,)),
            pltpu.SemaphoreType.DMA((1 + 2 * ITERS,)),
        ],
        compiler_params=pltpu.CompilerParams(
            collective_id=0, has_side_effects=True, vmem_limit_bytes=56 * 1024 * 1024
        ),
        name="pfasst",
    )(
        fine_cols.reshape((-1,)),
        coarse_cols.reshape((-1,)),
        init,
        rate,
        weight_parts(fine_tiles),
        weight_parts(coarse_tiles),
        widen(fine_halo),
        widen(coarse_halo),
        widen(owner),
        mapping,
    )
    return result.reshape((nb, 2, per, LANES)).transpose((2, 1, 0, 3)).reshape((per, 2, -1))


def solution(mesh):
    return jax.shard_map(
        functools.partial(per_device, mesh.shape["node"], mesh.shape["tm"]),
        mesh=mesh,
        in_specs=(
            P("parts", "node"),
            P("node"),
            P("node"),
            P("node", None, None, None),
            P("node", None),
            P("node"),
            P("node", None, None, None),
            P("node", None),
            P("node"),
            P("node"),
        ),
        out_specs=P("tm", "parts", "node"),
        check_vma=False,
    )
```

```python
import functools
import jax
import jax.numpy as jnp
from jax import lax
from jax.experimental import pallas as pl
from jax.experimental.pallas import tpu as pltpu
from jax.sharding import PartitionSpec as P

SLICES = 8
ITERS = 2
LANES = 128
ROWS = 8
DT = 0.125
QUAD = ((5.0 / 96.0, 1.0 / 12.0, -1.0 / 96.0), (-1.0 / 96.0, 1.0 / 12.0, 5.0 / 96.0))

f32 = jnp.float32
bf16 = jnp.bfloat16


def take(block, lane):
    return jnp.take_along_axis(block, lane, axis=1, mode="promise_in_bounds")


def species_mask():
    return lax.broadcasted_iota(jnp.int32, (ROWS, LANES), 0) < ROWS // 2


def explicit(x, product, source):
    is_u = species_mask()
    other = pltpu.roll(x, ROWS // 2, 0)
    growth = x * other * jnp.where(is_u, other, x)
    laplacian = product - 1.5 * x
    return jnp.where(is_u, laplacian - growth, 0.5 * laplacian + growth) + source


class Level:
    def __init__(self, count, rim, cols, weights, rim_index):
        self.count = count
        self.rim = rim
        self.cols = cols
        self.weights = weights
        self.rim_index = rim_index


def rim_copies(level, ext, send, send_sem, recv_sem, node):
    rim, count = level.rim, level.count
    down = pltpu.make_async_remote_copy(
        src_ref=send.at[pl.ds(0, rim)],
        dst_ref=ext.at[pl.ds(rim + count, rim)],
        send_sem=send_sem.at[0],
        recv_sem=recv_sem.at[0],
        device_id={"node": node - 1},
        device_id_type=pl.DeviceIdType.MESH,
    )
    up = pltpu.make_async_remote_copy(
        src_ref=send.at[pl.ds(rim, rim)],
        dst_ref=ext.at[pl.ds(0, rim)],
        send_sem=send_sem.at[1],
        recv_sem=recv_sem.at[1],
        device_id={"node": node + 1},
        device_id_type=pl.DeviceIdType.MESH,
    )
    return down, up


def gather_rim(level, ext, send, side, groups):
    rim, count = level.rim, level.count
    reach = min(2 * rim, count)
    first = 0 if side == 0 else count - reach

    def body(step, carry):
        place = side * rim + step
        index = jnp.broadcast_to(level.rim_index[pl.ds(place, 1), :], (ROWS, LANES))
        lane = index & (LANES - 1)
        owner = index >> 7
        for group in range(groups):
            rows = pl.ds(group * ROWS, ROWS)
            found = take(ext[rim + first, rows, :], lane)
            for block in range(first + 1, first + reach):
                found = jnp.where(owner == block, take(ext[rim + block, rows, :], lane), found)
            send[place, rows, :] = found
        return carry

    if rim <= 3:
        for step in range(rim):
            body(step, 0)
    else:
        lax.fori_loop(0, rim, body, 0)


def start_rims(level, ext, send, send_sem, recv_sem, node, nodes):
    groups = ext.shape[1] // ROWS
    down, up = rim_copies(level, ext, send, send_sem, recv_sem, node)
    gather_rim(level, ext, send, 0, groups)
    pl.when(node > 0)(lambda: down.start())
    gather_rim(level, ext, send, 1, groups)
    pl.when(node < nodes - 1)(lambda: up.start())


def multiply(x, weights):
    rows = x.shape[0]
    high = x.astype(bf16).astype(f32)
    both = jnp.concatenate([high, x - high], axis=0).astype(bf16)
    wide = lax.dot_general(both, weights, (((1,), (1,)), ((), ())), preferred_element_type=f32)
    return wide[:rows, :LANES] + wide[:rows, LANES:] + wide[rows:, :LANES]


def finish_rims(level, ext, send, send_sem, recv_sem, node, nodes, own, emit, meanwhile=None):
    down, up = rim_copies(level, ext, send, send_sem, recv_sem, node)
    rows = ext.shape[1]
    batch = 8 if level.count > 8 else level.count

    def own_product(r):
        return multiply(ext[level.rim + r], level.weights[r, :, 0:LANES])

    def product(r):
        x = jnp.concatenate([ext[level.cols[r, s]] for s in range(1, 3)], axis=1)
        return multiply(x, level.weights[r, :, LANES:])

    def over_batches(function):
        if level.count == batch:
            function(0)
        else:
            def body(step, carry):
                function(step * batch)
                return carry

            lax.fori_loop(0, level.count // batch, body, 0)

    def all_own(first):
        values = [own_product(first + i) for i in range(batch)]
        for i in range(batch):
            own[first + i, 0:rows] = values[i]

    def all_rest(first):
        values = [product(first + i) + own[first + i, 0:rows] for i in range(batch)]
        for i in range(batch):
            emit(first + i, values[i])

    over_batches(all_own)
    if meanwhile is not None:
        meanwhile()
    pl.when(node < nodes - 1)(lambda: down.wait_recv())
    pl.when(node > 0)(lambda: up.wait_recv())
    over_batches(all_rest)
    pl.when(node > 0)(lambda: down.wait_send())
    pl.when(node < nodes - 1)(lambda: up.wait_send())


def kernel(
    nodes,
    tms,
    cols_f,
    cols_c,
    initial,
    feed,
    kill,
    tiles_f,
    tiles_c,
    rim_f,
    rim_c,
    children,
    out,
    ext_a,
    ext_b,
    ext_c,
    ext_d,
    ext_0,
    ext_1,
    send_a,
    send_b,
    send_c,
    send_d,
    send_0,
    send_1,
    send_sem,
    recv_sem,
    state,
    terms,
    lhs,
    coarse_rate,
    base,
    fixed,
    coarse_w,
    results,
    end_coarse,
    got_coarse,
    end_fine,
    got_fine,
    tm_send,
    tm_recv,
    end_terms,
    got_terms,
    first_terms,
    starts,
    init,
    rate,
    raw_f,
    raw_c,
    w_f,
    w_c,
    mapping,
    owners,
    own,
    load_sem,
):
    node = lax.axis_index("node")
    tm = lax.axis_index("tm")
    per = ROWS // 2
    nb = init.shape[0]
    nbc = coarse_rate.shape[0]
    fine = Level(nb, rim_f.shape[0] // 2, cols_f, w_f, rim_f)
    coarse = Level(nbc, rim_c.shape[0] // 2, cols_c, w_c, rim_c)

    parts = 2 * per
    chunk = nb // parts

    def load_fine(part):
        rows = pl.ds(part * chunk, chunk)
        return pltpu.make_async_copy(tiles_f.at[rows], raw_f.at[rows], load_sem.at[part])

    load_coarse = pltpu.make_async_copy(tiles_c, raw_c, load_sem.at[parts])
    load_coarse.start()
    for part in range(parts):
        load_fine(part).start()

    barrier = pltpu.get_barrier_semaphore()

    def greet(axis, position, size):
        for offset in (-1, 1):
            other = position + offset

            @pl.when((other >= 0) & (other < size))
            def _():
                pl.semaphore_signal(
                    barrier, inc=1, device_id={axis: other}, device_id_type=pl.DeviceIdType.MESH
                )

    greet("node", node, nodes)
    greet("tm", tm, tms)

    peers = sum(
        ((other >= 0) & (other < size)).astype(jnp.int32)
        for other, size in ((node - 1, nodes), (node + 1, nodes), (tm - 1, tms), (tm + 1, tms))
    )

    def split_tiles(raw, weights, r):
        for t in range(3):
            tile = raw[r, t]
            high = tile.astype(bf16)
            weights[r, 0:LANES, t * LANES : (t + 1) * LANES] = high
            weights[r, LANES : 2 * LANES, t * LANES : (t + 1) * LANES] = (
                tile - high.astype(f32)
            ).astype(bf16)

    def split_part(part):
        load_fine(part).wait()

        def body(i, carry):
            split_tiles(raw_f, w_f, part * chunk + i)
            return carry

        lax.fori_loop(0, chunk, body, 0)

    def place_children(c, halves):
        line = children[pl.ds(c, 1), :]
        owner_lane = lax.broadcasted_iota(jnp.int32, (nb, LANES), 1) >> 2
        match = (line >> 7) == lax.broadcasted_iota(jnp.int32, (nb, LANES), 0)
        left = jnp.concatenate(
            [jnp.where(match, c, 0), jnp.where(match, owner_lane, 0)], axis=0
        ).astype(f32).astype(bf16)
        right = jnp.where(
            (line & (LANES - 1)) == lax.broadcasted_iota(jnp.int32, (LANES, LANES), 0), 1.0, 0.0
        ).astype(bf16)
        return halves + lax.dot_general(
            left, right, (((1,), (1,)), ((), ())), preferred_element_type=f32
        )

    halves = lax.fori_loop(
        0, nb, place_children, jnp.zeros((2 * nb, LANES), f32), unroll=4
    ).astype(jnp.int32)
    owner_of = halves[:nb] * (LANES // 4) + halves[nb:]
    ordinals = lax.broadcasted_iota(jnp.int32, (mapping.shape[0], LANES), 0)
    for b in range(nb):
        line = owner_of[b : b + 1]
        owners[b] = jnp.broadcast_to(line, (ROWS, LANES))
        mapping[:, b * LANES : (b + 1) * LANES] = jnp.where(ordinals == line, 0.25, 0.0).astype(bf16)
    for b in range(nb):
        lanes = slice(b * LANES, (b + 1) * LANES)
        u = jnp.broadcast_to(initial[0:1, lanes], (ROWS, LANES))
        v = jnp.broadcast_to(initial[1:2, lanes], (ROWS, LANES))
        init[b] = jnp.where(species_mask(), u, v)
        f = jnp.broadcast_to(feed[b : b + 1, :], (ROWS, LANES))
        k = jnp.broadcast_to(kill[b : b + 1, :], (ROWS, LANES))
        rate[b] = jnp.where(species_mask(), f, f + k)
    load_coarse.wait()
    for b in range(nbc):
        split_tiles(raw_c, w_c, b)
    pl.semaphore_wait(barrier, peers)

    is_u = species_mask()
    row = lax.broadcasted_iota(jnp.int32, (ROWS, LANES), 0)
    slice_of = row & (per - 1)

    def restrict(pieces, write):
        count = len(pieces)

        def body(b, carry):
            lanes = pl.ds(pl.multiple_of(b * LANES, LANES), LANES)
            for g in range(count):
                x = pieces[g](b)
                high = x.astype(bf16).astype(f32)
                lhs[pl.ds(16 * g, 16), lanes] = jnp.concatenate([high, x - high], axis=0).astype(bf16)
            return carry

        lax.fori_loop(0, nb, body, 0, unroll=2)
        summed = lax.dot_general(
            lhs[pl.ds(0, 16 * count), :],
            mapping[...],
            (((1,), (1,)), ((), ())),
            preferred_element_type=f32,
        )
        for g in range(count):
            both = summed[16 * g : 16 * g + 8] + summed[16 * g + 8 : 16 * g + 16]
            for b in range(nbc):
                write(g, b, both[:, b * LANES : (b + 1) * LANES])

    def prolong(z, d):
        index = owners[d]
        lane = index & (LANES - 1)
        owner = index >> 7
        found = take(z[0], lane)
        for b in range(1, nbc):
            found = jnp.where(owner == b, take(z[b], lane), found)
        return found

    def coarse_source(b):
        return jnp.where(is_u, coarse_rate[b], 0.0)

    def fine_source(b):
        return jnp.where(is_u, rate[b], 0.0)

    def begin(level, ext, send, sem):
        start_rims(level, ext, send, send_sem.at[sem], recv_sem.at[sem], node, nodes)

    def finish(level, ext, send, sem, emit, meanwhile=None):
        finish_rims(
            level, ext, send, send_sem.at[sem], recv_sem.at[sem], node, nodes, own, emit, meanwhile
        )

    def tm_copy(source, target, slot, sem):
        return pltpu.make_async_remote_copy(
            src_ref=source.at[slot],
            dst_ref=target.at[slot],
            send_sem=tm_send.at[sem],
            recv_sem=tm_recv.at[sem],
            device_id={"tm": tm + 1},
            device_id_type=pl.DeviceIdType.MESH,
        )

    def chain(number, start, has_fixed):
        copy = tm_copy(end_coarse, got_coarse, number, number)
        pl.when(tm > 0)(lambda: copy.wait_recv())
        for b in range(nbc):
            ext_0[coarse.rim + b] = jnp.where(tm == 0, start[b], got_coarse[number, b])

        def slice_body(s, carry):
            for m, (ext, send, sem, target) in enumerate(
                ((ext_0, send_0, 4, ext_1), (ext_1, send_1, 5, ext_0))
            ):
                def emit(b, product, m=m, ext=ext, target=target):
                    y = ext[coarse.rim + b]
                    value = y + DT * explicit(y, product, coarse_source(b))
                    if has_fixed:
                        value = value + fixed[m, b]
                    value = value / (1.0 + DT * coarse_rate[b])
                    results[m, b] = jnp.where(slice_of == s, value, results[m, b])
                    target[coarse.rim + b] = value if m == 0 else pltpu.roll(value, 1, 0)

                begin(coarse, ext, send, sem)
                finish(
                    coarse, ext, send, sem, emit, None if has_fixed else lambda m=m: split_part(2 * s + m)
                )
            return carry

        lax.fori_loop(0, per, slice_body, 0)

        @pl.when(tm < tms - 1)
        def _():
            for b in range(nbc):
                end_coarse[number, b] = pltpu.roll(results[1, b], ROWS - (per - 1), 0)
            copy.start()

    def finish_chain(number):
        copy = tm_copy(end_coarse, got_coarse, number, number)
        pl.when(tm < tms - 1)(lambda: copy.wait_send())

    results[...] = jnp.zeros_like(results)
    for ext, rim in (
        (ext_a, fine.rim), (ext_b, fine.rim), (ext_c, fine.rim),
        (ext_d, coarse.rim), (ext_0, coarse.rim), (ext_1, coarse.rim),
    ):
        @pl.when(node == 0)
        def _(ext=ext, rim=rim):
            ext[pl.ds(0, rim)] = jnp.zeros((rim,) + ext.shape[1:], f32)

        @pl.when(node == nodes - 1)
        def _(ext=ext, rim=rim):
            ext[pl.ds(ext.shape[0] - rim, rim)] = jnp.zeros((rim,) + ext.shape[1:], f32)

    def write_base(g, b, value):
        if g == 0:
            coarse_rate[b] = value
        else:
            base[b] = value

    restrict([lambda b: rate[b], lambda b: init[b]], write_base)
    for b in range(nb):
        ext_b[fine.rim + b] = init[b]
    begin(fine, ext_b, send_b, 1)
    chain(0, base, False)
    finish_chain(0)

    def emit_first(r, product):
        first_terms[r] = explicit(init[r], product, fine_source(r))

    finish(fine, ext_b, send_b, 1, emit_first)

    def first_states(d, carry):
        for m in range(2):
            z = [results[m, b] - base[b] for b in range(nbc)]
            state[m, d] = init[d] + prolong(z, d)
        return carry

    lax.fori_loop(0, nb, first_states, 0)

    def iterate(it, carry):
        copy = tm_copy(end_fine, got_fine, it, 3 + it)

        @pl.when(tm < tms - 1)
        def _():
            def body(b, c):
                end_fine[it, b] = pltpu.roll(state[1, b], ROWS - (per - 1), 0)
                return c

            lax.fori_loop(0, nb, body, 0, unroll=4)
            copy.start()

        def prepare(b, c):
            place = fine.rim + b
            ext_a[place, 0:8] = state[0, b]
            ext_a[place, 8:16] = state[1, b]
            return c

        lax.fori_loop(0, nb, prepare, 0, unroll=4)
        begin(fine, ext_a, send_a, 0)
        term_copy = tm_copy(end_terms, got_terms, it, 3 + ITERS + it)

        @pl.when(tm > 0)
        def _():
            copy.wait_recv()
            term_copy.wait_recv()

        def emit_a(r, product):
            source = fine_source(r)
            decay = rate[r]
            u1, u2 = state[0, r], state[1, r]
            f1 = explicit(u1, product[0:8], source)
            f2 = explicit(u2, product[8:16], source)
            end_terms[it, r] = pltpu.roll(f2, ROWS - (per - 1), 0)
            first_u = jnp.where(tm == 0, init[r], got_fine[it, r])
            first_f = jnp.where(tm == 0, first_terms[r], got_terms[it, r])
            u0 = jnp.where(slice_of == 0, first_u, pltpu.roll(u2, 1, 0))
            f0 = jnp.where(slice_of == 0, first_f, pltpu.roll(f2, 1, 0))
            g = [f0 - decay * u0, f1 - decay * u1, f2 - decay * u2]
            q = [sum(w * v for w, v in zip(weights, g)) for weights in QUAD]
            ext_b[fine.rim + r] = (u0 + DT * decay * u1 + q[0]) / (1.0 + DT * decay)
            starts[r] = u0
            terms[0, r] = g[0]
            terms[1, r] = DT * decay * u2 + q[1] - DT * f1

        finish(fine, ext_a, send_a, 0, emit_a)

        @pl.when(tm < tms - 1)
        def _():
            term_copy.start()
            copy.wait_send()

        def emit_b(r, product):
            decay = rate[r]
            v = ext_b[fine.rim + r]
            e = explicit(v, product, fine_source(r))
            ext_c[fine.rim + r] = (v + DT * e + terms[1, r]) / (1.0 + DT * decay)
            terms[1, r] = e - decay * v

        begin(fine, ext_b, send_b, 1)
        finish(fine, ext_b, send_b, 1, emit_b)

        def emit_c(r, product):
            v = ext_c[fine.rim + r]
            terms[2, r] = explicit(v, product, fine_source(r)) - rate[r] * v

        def quad_piece(weights):
            return lambda b: sum(w * terms[m, b] for m, w in enumerate(weights))

        def write_early(g, b, value):
            ext_d[coarse.rim + b, 8 * g : 8 * g + 8] = value
            coarse_w[g, b] = value

        def write_late(g, b, value):
            if g == 0:
                coarse_w[2, b] = value
            else:
                fixed[g - 1, b] = value

        def early():
            restrict([lambda b: starts[b], lambda b: ext_b[fine.rim + b]], write_early)
            begin(coarse, ext_d, send_d, 3)

        def emit_d(b, product):
            source = coarse_source(b)
            for m in range(2):
                e = explicit(coarse_w[m, b], product[8 * m : 8 * m + 8], source)
                fixed[m, b] = fixed[m, b] + DT * (coarse_rate[b] * coarse_w[m + 1, b] - e)

        begin(fine, ext_c, send_c, 2)
        finish(fine, ext_c, send_c, 2, emit_c, early)
        restrict(
            [lambda b: ext_c[fine.rim + b], quad_piece(QUAD[0]), quad_piece(QUAD[1])], write_late
        )
        finish(coarse, ext_d, send_d, 3, emit_d)
        pl.when(tm < tms - 1)(lambda: term_copy.wait_send())
        chain(1 + it, coarse_w.at[0], True)
        finish_chain(1 + it)

        def new_states(d, c):
            z = [results[1, b] - coarse_w[2, b] for b in range(nbc)]
            state[1, d] = ext_c[fine.rim + d] + prolong(z, d)
            z = [results[0, b] - coarse_w[1, b] for b in range(nbc)]
            state[0, d] = ext_b[fine.rim + d] + prolong(z, d)
            return c

        lax.fori_loop(0, nb, new_states, 0)
        return carry

    lax.fori_loop(0, ITERS, iterate, 0)
    for b in range(nb):
        out[:, b * LANES : (b + 1) * LANES] = state[1, b]


def per_device(
    nodes,
    tms,
    initial_fields,
    feed_rate,
    kill_rate,
    fine_tiles,
    fine_cols,
    fine_halo,
    coarse_tiles,
    coarse_cols,
    coarse_halo,
    children,
):
    per = SLICES // tms
    nb, nbc = fine_tiles.shape[0], coarse_tiles.shape[0]
    hb, hbc = fine_halo.shape[0] // (2 * LANES), coarse_halo.shape[0] // (2 * LANES)
    count = children.shape[0]
    vmem = pl.BlockSpec(memory_space=pltpu.VMEM)
    smem = pl.BlockSpec(memory_space=pltpu.SMEM)
    fine_ext, coarse_ext = nb + 2 * hb, nbc + 2 * hbc

    def scratch(*shape):
        return pltpu.VMEM(shape + (LANES,), f32)

    anywhere = pl.BlockSpec(memory_space=pl.ANY)
    result = pl.pallas_call(
        functools.partial(kernel, nodes, tms),
        out_shape=jax.ShapeDtypeStruct((ROWS, count), f32),
        in_specs=[smem, smem, vmem, vmem, vmem, anywhere, anywhere, vmem, vmem, vmem],
        out_specs=vmem,
        scratch_shapes=[
            scratch(fine_ext, 16),
            scratch(fine_ext, 8),
            scratch(fine_ext, 8),
            scratch(coarse_ext, 16),
            scratch(coarse_ext, 8),
            scratch(coarse_ext, 8),
            scratch(2 * hb, 16),
            scratch(2 * hb, 8),
            scratch(2 * hb, 8),
            scratch(2 * hbc, 16),
            scratch(2 * hbc, 8),
            scratch(2 * hbc, 8),
            pltpu.SemaphoreType.DMA((6, 2)),
            pltpu.SemaphoreType.DMA((6, 2)),
            scratch(2, nb, ROWS),
            scratch(3, nb, ROWS),
            pltpu.VMEM((80, count), bf16),
            scratch(nbc, ROWS),
            scratch(nbc, ROWS),
            scratch(2, nbc, ROWS),
            scratch(3, nbc, ROWS),
            scratch(2, nbc, ROWS),
            scratch(1 + ITERS, nbc, ROWS),
            scratch(1 + ITERS, nbc, ROWS),
            scratch(ITERS, nb, ROWS),
            scratch(ITERS, nb, ROWS),
            pltpu.SemaphoreType.DMA((1 + 3 * ITERS,)),
            pltpu.SemaphoreType.DMA((1 + 3 * ITERS,)),
            scratch(ITERS, nb, ROWS),
            scratch(ITERS, nb, ROWS),
            scratch(nb, ROWS),
            scratch(nb, ROWS),
            scratch(nb, ROWS),
            scratch(nb, ROWS),
            scratch(nb, 3, LANES),
            scratch(nbc, 3, LANES),
            pltpu.VMEM((nb, 2 * LANES, 3 * LANES), bf16),
            pltpu.VMEM((nbc, 2 * LANES, 3 * LANES), bf16),
            pltpu.VMEM((count // 4, count), bf16),
            pltpu.VMEM((nb, ROWS, LANES), jnp.int32),
            scratch(nb, 2 * ROWS),
            pltpu.SemaphoreType.DMA((2 * per + 1,)),
        ],
        compiler_params=pltpu.CompilerParams(
            collective_id=0, has_side_effects=True, vmem_limit_bytes=56 * 1024 * 1024
        ),
        name="pfasst",
    )(
        fine_cols,
        coarse_cols,
        initial_fields,
        feed_rate.reshape((nb, LANES)),
        kill_rate.reshape((nb, LANES)),
        fine_tiles,
        coarse_tiles,
        fine_halo.reshape((-1, LANES)),
        coarse_halo.reshape((-1, LANES)),
        children.reshape((nb, LANES)),
    )
    return result.reshape((2, per, count)).transpose((1, 0, 2))


def solution(mesh):
    return jax.shard_map(
        functools.partial(per_device, mesh.shape["node"], mesh.shape["tm"]),
        mesh=mesh,
        in_specs=(
            P("parts", "node"),
            P("node"),
            P("node"),
            P("node", None, None, None),
            P("node", None),
            P("node"),
            P("node", None, None, None),
            P("node", None),
            P("node"),
            P("node"),
        ),
        out_specs=P("tm", "parts", "node"),
        check_vma=False,
    )
```

```python
import functools
import jax
import jax.numpy as jnp
from jax import lax
from jax.experimental import pallas as pl
from jax.experimental.pallas import tpu as pltpu
from jax.sharding import PartitionSpec as P

SLICES = 8
ITERS = 2
LANES = 128
ROWS = 8
DT = 0.125
QUAD = ((5.0 / 96.0, 1.0 / 12.0, -1.0 / 96.0), (-1.0 / 96.0, 1.0 / 12.0, 5.0 / 96.0))

f32 = jnp.float32
bf16 = jnp.bfloat16


def take(block, lane):
    return jnp.take_along_axis(block, lane, axis=1, mode="promise_in_bounds")


def species_mask():
    return lax.broadcasted_iota(jnp.int32, (ROWS, LANES), 0) < ROWS // 2


def explicit(x, product, source):
    is_u = species_mask()
    other = pltpu.roll(x, ROWS // 2, 0)
    growth = x * other * jnp.where(is_u, other, x)
    laplacian = product - 1.5 * x
    return jnp.where(is_u, laplacian - growth, 0.5 * laplacian + growth) + source


class Level:
    def __init__(self, count, rim, cols, weights, rim_index):
        self.count = count
        self.rim = rim
        self.cols = cols
        self.weights = weights
        self.rim_index = rim_index


def rim_copies(level, ext, send, send_sem, recv_sem, node):
    rim, count = level.rim, level.count
    down = pltpu.make_async_remote_copy(
        src_ref=send.at[pl.ds(0, rim)],
        dst_ref=ext.at[pl.ds(rim + count, rim)],
        send_sem=send_sem.at[0],
        recv_sem=recv_sem.at[0],
        device_id={"node": node - 1},
        device_id_type=pl.DeviceIdType.MESH,
    )
    up = pltpu.make_async_remote_copy(
        src_ref=send.at[pl.ds(rim, rim)],
        dst_ref=ext.at[pl.ds(0, rim)],
        send_sem=send_sem.at[1],
        recv_sem=recv_sem.at[1],
        device_id={"node": node + 1},
        device_id_type=pl.DeviceIdType.MESH,
    )
    return down, up


def gather_rim(level, ext, send, side, groups):
    rim, count = level.rim, level.count
    reach = min(2 * rim, count)
    first = 0 if side == 0 else count - reach

    def body(step, carry):
        place = side * rim + step
        index = jnp.broadcast_to(level.rim_index[pl.ds(place, 1), :], (ROWS, LANES))
        lane = index & (LANES - 1)
        owner = index >> 7
        for group in range(groups):
            rows = pl.ds(group * ROWS, ROWS)
            found = take(ext[rim + first, rows, :], lane)
            for block in range(first + 1, first + reach):
                found = jnp.where(owner == block, take(ext[rim + block, rows, :], lane), found)
            send[place, rows, :] = found
        return carry

    if rim <= 3:
        for step in range(rim):
            body(step, 0)
    else:
        lax.fori_loop(0, rim, body, 0)


def start_rims(level, ext, send, send_sem, recv_sem, node, nodes):
    groups = ext.shape[1] // ROWS
    down, up = rim_copies(level, ext, send, send_sem, recv_sem, node)
    gather_rim(level, ext, send, 0, groups)
    pl.when(node > 0)(lambda: down.start())
    gather_rim(level, ext, send, 1, groups)
    pl.when(node < nodes - 1)(lambda: up.start())


def multiply(x, weights):
    rows = x.shape[0]
    high = x.astype(bf16).astype(f32)
    both = jnp.concatenate([high, x - high], axis=0).astype(bf16)
    wide = jnp.dot(both, weights, preferred_element_type=f32)
    return wide[:rows, :LANES] + wide[:rows, LANES:] + wide[rows:, :LANES]


def finish_rims(level, ext, send, send_sem, recv_sem, node, nodes, own, emit, meanwhile=None):
    down, up = rim_copies(level, ext, send, send_sem, recv_sem, node)
    rows = ext.shape[1]
    batch = 8 if level.count > 8 else level.count

    def own_product(r):
        return multiply(ext[level.rim + r], level.weights[r, 0:LANES, :])

    def product(r):
        x = jnp.concatenate([ext[level.cols[r, s]] for s in range(1, 3)], axis=1)
        return multiply(x, level.weights[r, LANES:, :])

    def over_batches(function):
        if level.count == batch:
            function(0)
        else:
            def body(step, carry):
                function(step * batch)
                return carry

            lax.fori_loop(0, level.count // batch, body, 0)

    def all_own(first):
        values = [own_product(first + i) for i in range(batch)]
        for i in range(batch):
            own[first + i, 0:rows] = values[i]

    def all_rest(first):
        values = [product(first + i) + own[first + i, 0:rows] for i in range(batch)]
        for i in range(batch):
            emit(first + i, values[i])

    over_batches(all_own)
    if meanwhile is not None:
        meanwhile()
    pl.when(node < nodes - 1)(lambda: down.wait_recv())
    pl.when(node > 0)(lambda: up.wait_recv())
    over_batches(all_rest)


def settle_rims(level, ext, send, send_sem, recv_sem, node, nodes):
    down, up = rim_copies(level, ext, send, send_sem, recv_sem, node)
    pl.when(node > 0)(lambda: down.wait_send())
    pl.when(node < nodes - 1)(lambda: up.wait_send())


def kernel(
    nodes,
    tms,
    cols_f,
    cols_c,
    initial,
    feed,
    kill,
    tiles_f,
    tiles_c,
    rim_f,
    rim_c,
    children,
    out,
    ext_a,
    ext_b,
    ext_c,
    ext_d,
    ext_0,
    ext_1,
    send_a,
    send_b,
    send_c,
    send_d,
    send_0,
    send_1,
    send_sem,
    recv_sem,
    state,
    terms,
    lhs,
    coarse_rate,
    coarse_scale,
    base,
    fixed,
    coarse_w,
    results,
    end_coarse,
    got_coarse,
    end_fine,
    got_fine,
    tm_send,
    tm_recv,
    end_terms,
    got_terms,
    first_terms,
    starts,
    init,
    rate,
    raw_f,
    raw_c,
    w_f,
    w_c,
    mapping,
    owners,
    own,
    load_sem,
):
    node = lax.axis_index("node")
    tm = lax.axis_index("tm")
    per = ROWS // 2
    nb = init.shape[0]
    nbc = coarse_rate.shape[0]
    fine = Level(nb, rim_f.shape[0] // 2, cols_f, w_f, rim_f)
    coarse = Level(nbc, rim_c.shape[0] // 2, cols_c, w_c, rim_c)

    parts = 2 * per
    chunk = nb // parts

    def load_fine(part):
        rows = pl.ds(part * chunk, chunk)
        return pltpu.make_async_copy(tiles_f.at[rows], raw_f.at[rows], load_sem.at[part])

    load_coarse = pltpu.make_async_copy(tiles_c, raw_c, load_sem.at[parts])
    load_coarse.start()
    for part in range(parts):
        load_fine(part).start()

    barrier = pltpu.get_barrier_semaphore()

    def greet(axis, position, size):
        for offset in (-1, 1):
            other = position + offset

            @pl.when((other >= 0) & (other < size))
            def _():
                pl.semaphore_signal(
                    barrier, inc=1, device_id={axis: other}, device_id_type=pl.DeviceIdType.MESH
                )

    greet("node", node, nodes)
    greet("tm", tm, tms)

    peers = sum(
        ((other >= 0) & (other < size)).astype(jnp.int32)
        for other, size in ((node - 1, nodes), (node + 1, nodes), (tm - 1, tms), (tm + 1, tms))
    )

    def split_tiles(raw, weights, r):
        for t in range(3):
            tile = raw[r, t].T
            high = tile.astype(bf16)
            weights[r, t * LANES : (t + 1) * LANES, 0:LANES] = high
            weights[r, t * LANES : (t + 1) * LANES, LANES : 2 * LANES] = (
                tile - high.astype(f32)
            ).astype(bf16)

    def split_part(part):
        load_fine(part).wait()

        def body(i, carry):
            split_tiles(raw_f, w_f, part * chunk + i)
            return carry

        lax.fori_loop(0, chunk, body, 0)

    def place_children(c, halves):
        line = children[pl.ds(c, 1), :]
        owner_lane = lax.broadcasted_iota(jnp.int32, (nb, LANES), 1) >> 2
        match = (line >> 7) == lax.broadcasted_iota(jnp.int32, (nb, LANES), 0)
        left = jnp.concatenate(
            [jnp.where(match, c, 0), jnp.where(match, owner_lane, 0)], axis=0
        ).astype(f32).astype(bf16)
        right = jnp.where(
            (line & (LANES - 1)) == lax.broadcasted_iota(jnp.int32, (LANES, LANES), 0), 1.0, 0.0
        ).astype(bf16)
        return halves + lax.dot_general(
            left, right, (((1,), (1,)), ((), ())), preferred_element_type=f32
        )

    halves = lax.fori_loop(0, nb, place_children, jnp.zeros((2 * nb, LANES), f32), unroll=4)
    owner_of = halves[:nb] * (LANES // 4) + halves[nb:]
    ordinals = lax.broadcasted_iota(jnp.int32, (LANES, LANES), 1).astype(f32)
    for b in range(nb):
        line = owner_of[b : b + 1]
        owners[b] = jnp.broadcast_to(line, (ROWS, LANES)).astype(jnp.int32)
        column = jnp.broadcast_to(line, (LANES, LANES)).T
        for n in range(nbc):
            mapping[b * LANES : (b + 1) * LANES, n * LANES : (n + 1) * LANES] = jnp.where(
                column == ordinals + float(n * LANES), 0.25, 0.0
            ).astype(bf16)
    for b in range(nb):
        lanes = slice(b * LANES, (b + 1) * LANES)
        u = jnp.broadcast_to(initial[0:1, lanes], (ROWS, LANES))
        v = jnp.broadcast_to(initial[1:2, lanes], (ROWS, LANES))
        init[b] = jnp.where(species_mask(), u, v)
        f = jnp.broadcast_to(feed[b : b + 1, :], (ROWS, LANES))
        k = jnp.broadcast_to(kill[b : b + 1, :], (ROWS, LANES))
        rate[b] = jnp.where(species_mask(), f, f + k)
    load_coarse.wait()
    for b in range(nbc):
        split_tiles(raw_c, w_c, b)
    pl.semaphore_wait(barrier, peers)

    is_u = species_mask()
    row = lax.broadcasted_iota(jnp.int32, (ROWS, LANES), 0)
    slice_of = row & (per - 1)

    def restrict(pieces, write):
        count = len(pieces)

        def body(b, carry):
            lanes = pl.ds(pl.multiple_of(b * LANES, LANES), LANES)
            for g in range(count):
                x = pieces[g](b)
                high = x.astype(bf16).astype(f32)
                lhs[pl.ds(16 * g, 16), lanes] = jnp.concatenate([high, x - high], axis=0).astype(bf16)
            return carry

        lax.fori_loop(0, nb, body, 0, unroll=2)
        summed = jnp.dot(lhs[pl.ds(0, 16 * count), :], mapping[...], preferred_element_type=f32)
        for g in range(count):
            both = summed[16 * g : 16 * g + 8] + summed[16 * g + 8 : 16 * g + 16]
            for b in range(nbc):
                write(g, b, both[:, b * LANES : (b + 1) * LANES])

    def prolong(z, d):
        index = owners[d]
        lane = index & (LANES - 1)
        owner = index >> 7
        found = take(z[0], lane)
        for b in range(1, nbc):
            found = jnp.where(owner == b, take(z[b], lane), found)
        return found

    def coarse_source(b):
        return jnp.where(is_u, coarse_rate[b], 0.0)

    def fine_source(b):
        return jnp.where(is_u, rate[b], 0.0)

    def begin(level, ext, send, sem):
        start_rims(level, ext, send, send_sem.at[sem], recv_sem.at[sem], node, nodes)

    def finish(level, ext, send, sem, emit, meanwhile=None):
        finish_rims(
            level, ext, send, send_sem.at[sem], recv_sem.at[sem], node, nodes, own, emit, meanwhile
        )

    def settle(level, ext, send, sem):
        settle_rims(level, ext, send, send_sem.at[sem], recv_sem.at[sem], node, nodes)

    def tm_copy(source, target, slot, sem):
        return pltpu.make_async_remote_copy(
            src_ref=source.at[slot],
            dst_ref=target.at[slot],
            send_sem=tm_send.at[sem],
            recv_sem=tm_recv.at[sem],
            device_id={"tm": tm + 1},
            device_id_type=pl.DeviceIdType.MESH,
        )

    def chain(number, start, has_fixed):
        copy = tm_copy(end_coarse, got_coarse, number, number)
        pl.when(tm > 0)(lambda: copy.wait_recv())
        for b in range(nbc):
            ext_0[coarse.rim + b] = jnp.where(tm == 0, start[b], got_coarse[number, b])

        def slice_body(s, carry):
            for m, (ext, send, sem, target) in enumerate(
                ((ext_0, send_0, 4, ext_1), (ext_1, send_1, 5, ext_0))
            ):
                def emit(b, product, m=m, ext=ext, target=target):
                    y = ext[coarse.rim + b]
                    value = y + DT * explicit(y, product, coarse_source(b))
                    if has_fixed:
                        value = value + fixed[m, b]
                    value = value * coarse_scale[b]
                    results[m, b] = jnp.where(slice_of == s, value, results[m, b])
                    target[coarse.rim + b] = value if m == 0 else pltpu.roll(value, 1, 0)

                begin(coarse, ext, send, sem)
                finish(
                    coarse, ext, send, sem, emit, None if has_fixed else lambda m=m: split_part(2 * s + m)
                )
                if m == 1:
                    settle(coarse, ext_0, send_0, 4)
                else:
                    pl.when(s > 0)(lambda: settle(coarse, ext_1, send_1, 5))
            return carry

        lax.fori_loop(0, per, slice_body, 0)

        @pl.when(tm < tms - 1)
        def _():
            for b in range(nbc):
                end_coarse[number, b] = pltpu.roll(results[1, b], ROWS - (per - 1), 0)
            copy.start()

        settle(coarse, ext_1, send_1, 5)

    def finish_chain(number):
        copy = tm_copy(end_coarse, got_coarse, number, number)
        pl.when(tm < tms - 1)(lambda: copy.wait_send())

    results[...] = jnp.zeros_like(results)
    for ext, rim in (
        (ext_a, fine.rim), (ext_b, fine.rim), (ext_c, fine.rim),
        (ext_d, coarse.rim), (ext_0, coarse.rim), (ext_1, coarse.rim),
    ):
        @pl.when(node == 0)
        def _(ext=ext, rim=rim):
            ext[pl.ds(0, rim)] = jnp.zeros((rim,) + ext.shape[1:], f32)

        @pl.when(node == nodes - 1)
        def _(ext=ext, rim=rim):
            ext[pl.ds(ext.shape[0] - rim, rim)] = jnp.zeros((rim,) + ext.shape[1:], f32)

    def write_base(g, b, value):
        if g == 0:
            coarse_rate[b] = value
            coarse_scale[b] = 1.0 / (1.0 + DT * value)
        else:
            base[b] = value

    restrict([lambda b: rate[b], lambda b: init[b]], write_base)
    for b in range(nb):
        ext_b[fine.rim + b] = init[b]
    begin(fine, ext_b, send_b, 1)
    chain(0, base, False)
    finish_chain(0)

    def emit_first(r, product):
        first_terms[r] = explicit(init[r], product, fine_source(r))

    finish(fine, ext_b, send_b, 1, emit_first)
    settle(fine, ext_b, send_b, 1)

    def first_states(d, carry):
        for m in range(2):
            z = [results[m, b] - base[b] for b in range(nbc)]
            state[m, d] = init[d] + prolong(z, d)
        return carry

    lax.fori_loop(0, nb, first_states, 0)

    def iterate(it, carry):
        copy = tm_copy(end_fine, got_fine, it, 3 + it)

        @pl.when(tm < tms - 1)
        def _():
            def body(b, c):
                end_fine[it, b] = pltpu.roll(state[1, b], ROWS - (per - 1), 0)
                return c

            lax.fori_loop(0, nb, body, 0, unroll=4)
            copy.start()

        def prepare(b, c):
            place = fine.rim + b
            ext_a[place, 0:8] = state[0, b]
            ext_a[place, 8:16] = state[1, b]
            return c

        lax.fori_loop(0, nb, prepare, 0, unroll=4)
        begin(fine, ext_a, send_a, 0)
        term_copy = tm_copy(end_terms, got_terms, it, 3 + ITERS + it)

        @pl.when(tm > 0)
        def _():
            copy.wait_recv()
            term_copy.wait_recv()

        def emit_a(r, product):
            source = fine_source(r)
            decay = rate[r]
            u1, u2 = state[0, r], state[1, r]
            f1 = explicit(u1, product[0:8], source)
            f2 = explicit(u2, product[8:16], source)
            end_terms[it, r] = pltpu.roll(f2, ROWS - (per - 1), 0)
            first_u = jnp.where(tm == 0, init[r], got_fine[it, r])
            first_f = jnp.where(tm == 0, first_terms[r], got_terms[it, r])
            u0 = jnp.where(slice_of == 0, first_u, pltpu.roll(u2, 1, 0))
            f0 = jnp.where(slice_of == 0, first_f, pltpu.roll(f2, 1, 0))
            g = [f0 - decay * u0, f1 - decay * u1, f2 - decay * u2]
            q = [sum(w * v for w, v in zip(weights, g)) for weights in QUAD]
            ext_b[fine.rim + r] = (u0 + DT * decay * u1 + q[0]) / (1.0 + DT * decay)
            starts[r] = u0
            terms[0, r] = g[0]
            terms[1, r] = DT * decay * u2 + q[1] - DT * f1

        finish(fine, ext_a, send_a, 0, emit_a)

        @pl.when(tm < tms - 1)
        def _():
            term_copy.start()
            copy.wait_send()

        def emit_b(r, product):
            decay = rate[r]
            v = ext_b[fine.rim + r]
            e = explicit(v, product, fine_source(r))
            ext_c[fine.rim + r] = (v + DT * e + terms[1, r]) / (1.0 + DT * decay)
            terms[1, r] = e - decay * v

        begin(fine, ext_b, send_b, 1)
        finish(fine, ext_b, send_b, 1, emit_b)

        def emit_c(r, product):
            v = ext_c[fine.rim + r]
            terms[2, r] = explicit(v, product, fine_source(r)) - rate[r] * v

        def quad_piece(weights):
            return lambda b: sum(w * terms[m, b] for m, w in enumerate(weights))

        def write_early(g, b, value):
            ext_d[coarse.rim + b, 8 * g : 8 * g + 8] = value
            coarse_w[g, b] = value

        def write_late(g, b, value):
            if g == 0:
                coarse_w[2, b] = value
            else:
                fixed[g - 1, b] = value

        def early():
            restrict([lambda b: starts[b], lambda b: ext_b[fine.rim + b]], write_early)
            begin(coarse, ext_d, send_d, 3)

        def emit_d(b, product):
            source = coarse_source(b)
            for m in range(2):
                e = explicit(coarse_w[m, b], product[8 * m : 8 * m + 8], source)
                fixed[m, b] = fixed[m, b] + DT * (coarse_rate[b] * coarse_w[m + 1, b] - e)

        begin(fine, ext_c, send_c, 2)
        finish(fine, ext_c, send_c, 2, emit_c, early)
        restrict(
            [lambda b: ext_c[fine.rim + b], quad_piece(QUAD[0]), quad_piece(QUAD[1])], write_late
        )
        finish(coarse, ext_d, send_d, 3, emit_d)
        settle(fine, ext_a, send_a, 0)
        settle(fine, ext_b, send_b, 1)
        settle(fine, ext_c, send_c, 2)
        settle(coarse, ext_d, send_d, 3)
        pl.when(tm < tms - 1)(lambda: term_copy.wait_send())
        chain(1 + it, coarse_w.at[0], True)
        finish_chain(1 + it)

        def new_states(d, c):
            z = [results[1, b] - coarse_w[2, b] for b in range(nbc)]
            state[1, d] = ext_c[fine.rim + d] + prolong(z, d)
            z = [results[0, b] - coarse_w[1, b] for b in range(nbc)]
            state[0, d] = ext_b[fine.rim + d] + prolong(z, d)
            return c

        lax.fori_loop(0, nb, new_states, 0)
        return carry

    lax.fori_loop(0, ITERS, iterate, 0)
    for b in range(nb):
        out[:, b * LANES : (b + 1) * LANES] = state[1, b]


def per_device(
    nodes,
    tms,
    initial_fields,
    feed_rate,
    kill_rate,
    fine_tiles,
    fine_cols,
    fine_halo,
    coarse_tiles,
    coarse_cols,
    coarse_halo,
    children,
):
    per = SLICES // tms
    nb, nbc = fine_tiles.shape[0], coarse_tiles.shape[0]
    hb, hbc = fine_halo.shape[0] // (2 * LANES), coarse_halo.shape[0] // (2 * LANES)
    count = children.shape[0]
    vmem = pl.BlockSpec(memory_space=pltpu.VMEM)
    smem = pl.BlockSpec(memory_space=pltpu.SMEM)
    fine_ext, coarse_ext = nb + 2 * hb, nbc + 2 * hbc

    def scratch(*shape):
        return pltpu.VMEM(shape + (LANES,), f32)

    anywhere = pl.BlockSpec(memory_space=pl.ANY)
    result = pl.pallas_call(
        functools.partial(kernel, nodes, tms),
        out_shape=jax.ShapeDtypeStruct((ROWS, count), f32),
        in_specs=[smem, smem, vmem, vmem, vmem, anywhere, anywhere, vmem, vmem, vmem],
        out_specs=vmem,
        scratch_shapes=[
            scratch(fine_ext, 16),
            scratch(fine_ext, 8),
            scratch(fine_ext, 8),
            scratch(coarse_ext, 16),
            scratch(coarse_ext, 8),
            scratch(coarse_ext, 8),
            scratch(2 * hb, 16),
            scratch(2 * hb, 8),
            scratch(2 * hb, 8),
            scratch(2 * hbc, 16),
            scratch(2 * hbc, 8),
            scratch(2 * hbc, 8),
            pltpu.SemaphoreType.DMA((6, 2)),
            pltpu.SemaphoreType.DMA((6, 2)),
            scratch(2, nb, ROWS),
            scratch(3, nb, ROWS),
            pltpu.VMEM((80, count), bf16),
            scratch(nbc, ROWS),
            scratch(nbc, ROWS),
            scratch(nbc, ROWS),
            scratch(2, nbc, ROWS),
            scratch(3, nbc, ROWS),
            scratch(2, nbc, ROWS),
            scratch(1 + ITERS, nbc, ROWS),
            scratch(1 + ITERS, nbc, ROWS),
            scratch(ITERS, nb, ROWS),
            scratch(ITERS, nb, ROWS),
            pltpu.SemaphoreType.DMA((1 + 3 * ITERS,)),
            pltpu.SemaphoreType.DMA((1 + 3 * ITERS,)),
            scratch(ITERS, nb, ROWS),
            scratch(ITERS, nb, ROWS),
            scratch(nb, ROWS),
            scratch(nb, ROWS),
            scratch(nb, ROWS),
            scratch(nb, ROWS),
            scratch(nb, 3, LANES),
            scratch(nbc, 3, LANES),
            pltpu.VMEM((nb, 3 * LANES, 2 * LANES), bf16),
            pltpu.VMEM((nbc, 3 * LANES, 2 * LANES), bf16),
            pltpu.VMEM((count, count // 4), bf16),
            pltpu.VMEM((nb, ROWS, LANES), jnp.int32),
            scratch(nb, 2 * ROWS),
            pltpu.SemaphoreType.DMA((2 * per + 1,)),
        ],
        compiler_params=pltpu.CompilerParams(
            collective_id=0, has_side_effects=True, vmem_limit_bytes=56 * 1024 * 1024
        ),
        name="pfasst",
    )(
        fine_cols,
        coarse_cols,
        initial_fields,
        feed_rate.reshape((nb, LANES)),
        kill_rate.reshape((nb, LANES)),
        fine_tiles,
        coarse_tiles,
        fine_halo.reshape((-1, LANES)),
        coarse_halo.reshape((-1, LANES)),
        children.reshape((nb, LANES)),
    )
    return result.reshape((2, per, count)).transpose((1, 0, 2))


def solution(mesh):
    return jax.shard_map(
        functools.partial(per_device, mesh.shape["node"], mesh.shape["tm"]),
        mesh=mesh,
        in_specs=(
            P("parts", "node"),
            P("node"),
            P("node"),
            P("node", None, None, None),
            P("node", None),
            P("node"),
            P("node", None, None, None),
            P("node", None),
            P("node"),
            P("node"),
        ),
        out_specs=P("tm", "parts", "node"),
        check_vma=False,
    )
```
